32 devices in a mesh: seq: 4 (over z), exp: 8 (over y, x, core).
Axes of the slice: x: 2, y: 2, z: 4, core: 2. Of those that a mesh axis runs over, the one named last changes fastest.
Arguments:
- queries: bfloat16 [32, 4096], P('exp'), may hold values from -80 to 80
- new_kv: bfloat16 [2, 32, 512], P(None, 'exp'), may hold values from -4 to 4
- kv_cache: bfloat16 [2, 32, 2048, 512], P(None, 'exp', 'seq'), may hold values from -4 to 4
- lengths: int32 [32], P('exp'), may hold values from 1 to 2048, as said below
- out_proj: bfloat16 [4096, 2048], P('seq'), may hold values from -0.09375 to 0.09375
- hidden_in: float32 [32, 2048], P('exp'), may hold values from -6 to 6
- norm_gain: float32 [2048], replicated, may hold values from 0.1 to 1.9
- router: bfloat16 [2048, 32], replicated, may hold values from -0.125 to 0.125
- expert_ids: int32 [32, 8], replicated, may hold values from 0 to 31, all different within a row; in each aligned block of 32 rows (0 to 31, 32 to 63, ...) at most 16 rows name the same one
- w_gate_up: bfloat16 [32, 2048, 1536], P(('seq', 'exp')), may hold values from -0.125 to 0.125
- w_down: bfloat16 [32, 768, 2048], P(('seq', 'exp')), may hold values from -0.21875 to 0.21875
- talk_proj: bfloat16 [2048, 1024], replicated, may hold values from -0.125 to 0.125
- talk_gain: float32 [1024], replicated, may hold values from 0.1 to 1.9
- talk_router: bfloat16 [1024, 32], replicated, may hold values from -0.1875 to 0.1875
- talk_ids: int32 [32, 8], replicated, may hold values from 0 to 31, all different within a row; in each aligned block of 32 rows (0 to 31, 32 to 63, ...) at most 16 rows name the same one
- talk_gate_up: bfloat16 [32, 1024, 768], P(('seq', 'exp')), may hold values from -0.1875 to 0.1875
- talk_down: bfloat16 [32, 384, 1024], P(('seq', 'exp')), may hold values from -0.3125 to 0.3125
Outputs:
- thinker_out: float32 [32, 2048], P('exp')
- talker_out: float32 [32, 1024], P('exp')
The draws below stay inside these ranges and needn't reach their ends.
Inputs may be any that keep to these rules, and one draw needn't show every extreme that they name: `lengths`: some conversation uses all 2048 positions and some uses only one. `expert_ids`: each row names 8 different experts. Over all 32 rows no expert is named more than 16 times, and in every draw some expert is named exactly 16 times. `talk_ids`: as for expert_ids.
All inputs are finite; a program needn't handle non-finite values.
Results may differ from the reference program's by a relative error of at most 0.011.
Values may be sent and summed in bfloat16 or wider, within the bound.
A program may use at most 128 MiB of HBM per device.

```python
import math
import jax
import jax.numpy as jnp
import numpy as np
from jax import lax

D = 2048
H = 32
KVH = 4
HD = 128
FF = 768
TOP = 8
DT = 1024
FT = 384
EXPERTS = 32
CONVS = 32
CTX = 2048
CAP = 16


def shared_leading(key):
    return jnp.clip(jax.random.normal(jax.random.fold_in(key, 5), (CONVS, KVH * HD), jnp.float32), -4.0, 4.0)


def draw_kv_cache(key, part):
    leading = shared_leading(key)
    key = jax.random.fold_in(key, 11)
    entries = jnp.clip(jax.random.normal(key, (2, CONVS, CTX, KVH * HD), jnp.float32), -4.0, 4.0)
    entries = entries.at[0, :, 0, :].set(leading)
    direction = jax.random.uniform(jax.random.fold_in(key, 7), (CONVS, 1, KVH * HD), jnp.float32, -1.0, 1.0)
    position = (jnp.arange(CTX, dtype=jnp.float32) + 1.0) / CTX
    noise = 0.8 * entries[1]
    ramp = 0.1 + 1.9 * position
    values = jnp.clip(noise + ramp[None, :, None] * direction, -4.0, 4.0)
    entries = entries.at[1].set(values)
    return entries.astype(jnp.bfloat16)


def draw_queries(key, part):
    key = jax.random.fold_in(key, 23)
    values = jnp.clip(jax.random.normal(key, (CONVS, H * HD), jnp.float32), -4.0, 4.0)
    return values.astype(jnp.bfloat16)


def draw_lengths(key, part):
    key = jax.random.fold_in(key, 31)
    total_count = CONVS
    spans = jax.random.randint(jax.random.fold_in(key, 1), (total_count,), 1, CTX + 1, dtype=jnp.int32)
    longest = jax.random.randint(jax.random.fold_in(key, 2), (), 0, total_count, dtype=jnp.int32)
    offset = jax.random.randint(jax.random.fold_in(key, 3), (), 0, total_count - 1, dtype=jnp.int32)
    shortest = (longest + 1 + offset) % total_count
    spans = spans.at[longest].set(CTX).at[shortest].set(1)
    return spans


def block_levels(rng, extent, pieces, low, largest):
    def one(dim, shards_of):
        heights = jax.random.uniform(jax.random.fold_in(jax.random.fold_in(rng, 6), dim), (shards_of,), jnp.float32, low / len(pieces), largest / len(pieces))
        return jnp.repeat(jnp.exp(heights), extent[dim] // shards_of).reshape((-1,) + (1,) * (len(extent) - dim - 1))

    level = one(*pieces[0])
    for cut in pieces[1:]:
        level = level * one(*cut)
    return level


def deal_out(stream_key, own, number, rows, number_of, top, bound, slope):
    order = jax.random.permutation(stream_key, number_of)
    packed, usual = load_shares(number_of, rows * top, bound, slope, True), load_shares(number_of, rows * top, bound, slope, False)
    places = jnp.arange(number_of)

    def named(sizes, turn):
        used = int((sizes > 0).sum())
        fixed = max(1, used // 4)
        moved = fixed + (places - fixed + turn * (used - fixed)) % max(1, number_of - fixed)
        return jnp.zeros((number_of,), jnp.int32).at[order[jnp.where(places < fixed, places, moved)]].set(jnp.asarray(sizes, jnp.int32))

    sizes = jnp.where(number % 4 == 0, named(packed, number // 4), named(usual, number - number // 4 - 1))
    mixed = jax.random.permutation(jax.random.fold_in(own, 3), number_of)
    source_of, receiver = mixed[0:number_of // 2 * 2:2], mixed[1:number_of // 2 * 2:2]
    margin = jnp.minimum(sizes[source_of] - 1, bound - sizes[receiver]) // 2
    margin = jnp.where((source_of == order[0]) | (receiver == order[0]) | (sizes[receiver] == 0), 0, jnp.maximum(margin, 0))
    moved = jax.random.randint(jax.random.fold_in(own, 4), (number_of // 2,), 0, 1 << 20) % (margin + 1)
    sizes = sizes.at[source_of].add(-moved).at[receiver].add(moved)
    members = jnp.searchsorted(jnp.cumsum(sizes), jnp.arange(rows * top), side="right").astype(jnp.int32)
    grid = members.reshape(top, rows).T
    grid = grid[jax.random.permutation(jax.random.fold_in(own, 1), rows)]
    turn = jax.random.randint(jax.random.fold_in(own, 2), (rows, 1), 0, top)
    return jnp.take_along_axis(grid, (jnp.arange(top)[None, :] + turn) % top, axis=1)


def load_shares(number_of, total, limit, slope, full):
    portions = [(1 << 20) // math.isqrt(grade ** slope) + 1 for grade in range(1, number_of + 1)]
    largest = limit if full else min(limit, max(-(-total // number_of), total * portions[0] // sum(portions)))
    least = 1 if total - largest >= number_of - 1 else 0
    given, spare = [largest] + [least] * (number_of - 1), total - largest - least * (number_of - 1)
    while spare > 0:
        free = [i for i in range(1, number_of) if given[i] < largest] or [i for i in range(1, number_of) if given[i] < limit]
        pool, budget = sum([portions[i] for i in free]), spare
        for i in free:
            addition = min(limit - given[i], max(1, budget * portions[i] // pool), spare)
            given[i] = given[i] + addition
            spare = spare - addition
    return np.array(given)


def bell_draw(rng, extent, scale, limit, shards=(), kind=jnp.bfloat16):
    values = scale * jax.random.normal(rng, extent, jnp.float32)
    if shards:
        values = values * block_levels(rng, extent, shards, -0.22, 0.18)
    return jnp.clip(values, -limit, limit).astype(kind)


def setup_inputs(seed: int = 0) -> dict:
    splits = jax.random.split(jax.random.key(seed), 18)
    queries = draw_queries(jax.random.fold_in(splits[17], 71), 0)
    new_kv = bell_draw(splits[1], (2, CONVS, KVH * HD), 1.0, 4.0, ((1, 8),))
    kv_cache = draw_kv_cache(jax.random.fold_in(splits[17], 71), 0)
    lengths = draw_lengths(jax.random.fold_in(splits[17], 71), 0)
    out_proj = bell_draw(splits[4], (H * HD, D), (H * HD) ** -0.5, 0.09375, ((0, 4),))
    hidden_in = bell_draw(splits[5], (CONVS, D), 1.0, 6.0, ((0, 8),), jnp.float32)
    norm_gain = jnp.clip(1.0 + 0.18 * jax.random.normal(splits[6], (D,), jnp.float32), 0.1, 1.9)
    router = bell_draw(splits[7], (D, EXPERTS), D ** -0.5, 0.125)
    expert_ids_keys = jax.random.split(jax.random.fold_in(splits[8], 1), CONVS // CONVS)
    expert_ids_turns = jax.random.permutation(jax.random.fold_in(splits[8], 3), CONVS // CONVS)
    expert_ids = jax.vmap(lambda own, number: deal_out(jax.random.fold_in(splits[8], 2), own, number, CONVS, EXPERTS, TOP, CAP, 2))(expert_ids_keys, expert_ids_turns).reshape((CONVS, TOP))
    w_gate_up = bell_draw(splits[9], (EXPERTS, D, 2 * FF), D ** -0.5, 0.125, ((0, 32),))
    w_down = bell_draw(splits[10], (EXPERTS, FF, D), FF ** -0.5, 0.21875, ((0, 32),))
    talk_proj = bell_draw(splits[11], (D, DT), D ** -0.5, 0.125)
    talk_gain = jnp.clip(1.0 + 0.18 * jax.random.normal(splits[12], (DT,), jnp.float32), 0.1, 1.9)
    talk_router = bell_draw(splits[13], (DT, EXPERTS), DT ** -0.5, 0.1875)
    talk_ids_keys = jax.random.split(jax.random.fold_in(splits[14], 1), CONVS // CONVS)
    talk_ids_turns = jax.random.permutation(jax.random.fold_in(splits[14], 3), CONVS // CONVS)
    talk_ids = jax.vmap(lambda own, number: deal_out(jax.random.fold_in(splits[14], 2), own, number, CONVS, EXPERTS, TOP, CAP, 2))(talk_ids_keys, talk_ids_turns).reshape((CONVS, TOP))
    talk_gate_up = bell_draw(splits[15], (EXPERTS, DT, 2 * FT), DT ** -0.5, 0.1875, ((0, 32),))
    talk_down = bell_draw(splits[16], (EXPERTS, FT, DT), FT ** -0.5, 0.3125, ((0, 32),))
    return dict(queries=queries, new_kv=new_kv, kv_cache=kv_cache, lengths=lengths, out_proj=out_proj, hidden_in=hidden_in, norm_gain=norm_gain, router=router, expert_ids=expert_ids, w_gate_up=w_gate_up, w_down=w_down, talk_proj=talk_proj, talk_gain=talk_gain, talk_router=talk_router, talk_ids=talk_ids, talk_gate_up=talk_gate_up, talk_down=talk_down)


def attend_one(query_row, cached_keys, cached_values, fresh_key, fresh_value, length):
    groups = H // KVH
    query_f = query_row.reshape(KVH, groups, HD).astype(jnp.float32)
    keys = jnp.concatenate([cached_keys.reshape(CTX, KVH, HD), fresh_key.reshape(1, KVH, HD)], axis=0).astype(jnp.float32)
    values = jnp.concatenate([cached_values.reshape(CTX, KVH, HD), fresh_value.reshape(1, KVH, HD)], axis=0).astype(jnp.float32)
    scores = jnp.einsum('kjd,pkd->kjp', query_f, keys, precision=lax.Precision.HIGHEST) * HD ** (-0.5)
    valid = jnp.concatenate([jnp.arange(CTX, dtype=jnp.int32) < length, jnp.ones((1,), bool)], axis=0)
    scores = jnp.where(valid[None, None, :], scores, -jnp.inf)
    peak = lax.optimization_barrier(jnp.max(scores, axis=-1, keepdims=True))
    weights = jnp.exp(scores - peak)
    totals = lax.optimization_barrier(jnp.sum(weights, axis=-1))
    mixed = jnp.einsum('kjp,pkd->kjd', weights, values, precision=lax.Precision.HIGHEST)
    return (mixed / totals[..., None]).reshape(H * HD).astype(jnp.bfloat16)

def expert_layer(stream, gain, router_w, picks, gate_up, down_w):
    row_count, width = stream.shape
    top_count = picks.shape[1]
    inner_width = down_w.shape[1]
    normed = (stream * lax.rsqrt(lax.optimization_barrier(jnp.mean(stream * stream, axis=1, keepdims=True)) + 1e-06) * gain).astype(jnp.bfloat16)
    logits = jnp.dot(normed, router_w, preferred_element_type=jnp.float32)
    picked = jnp.take_along_axis(logits, picks, axis=1)
    sigmoids = jax.nn.sigmoid(picked)
    gates = sigmoids / lax.optimization_barrier(jnp.sum(sigmoids, axis=1, keepdims=True))
    flat_ids = picks.reshape(-1).astype(jnp.int32)

    def visit(totals, expert):
        hits = (flat_ids == expert).astype(jnp.int32)
        places = jnp.nonzero(flat_ids == expert, size=CAP, fill_value=0)[0].astype(jnp.int32)
        live = (jnp.arange(CAP, dtype=jnp.int32) < jnp.sum(hits)).astype(jnp.float32)
        chosen = normed[places // top_count]
        both = jnp.dot(chosen, gate_up[expert], preferred_element_type=jnp.float32)
        inner = (jax.nn.silu(both[:, :inner_width]) * both[:, inner_width:]).astype(jnp.bfloat16)
        replies = jnp.dot(inner, down_w[expert], preferred_element_type=jnp.float32).astype(jnp.bfloat16)
        replies = lax.optimization_barrier(replies).astype(jnp.float32)
        return (totals.at[places].add(replies * live[:, None]), None)
    start_totals = jnp.zeros((row_count * top_count, width), jnp.float32)
    totals, unused = lax.scan(visit, start_totals, jnp.arange(EXPERTS, dtype=jnp.int32))
    totals = totals.reshape(row_count, top_count, width)
    return stream + lax.optimization_barrier(jnp.sum(gates[:, :, None] * totals, axis=1))

def reference(queries, new_kv, kv_cache, lengths, out_proj, hidden_in, norm_gain, router, expert_ids, w_gate_up, w_down, talk_proj, talk_gain, talk_router, talk_ids, talk_gate_up, talk_down):

    def attend_items(items):
        return attend_one(items[0], items[1], items[2], items[3], items[4], items[5])
    attn = lax.map(attend_items, (queries, kv_cache[0], kv_cache[1], new_kv[0], new_kv[1], lengths))
    state = hidden_in + jnp.dot(attn, out_proj, preferred_element_type=jnp.float32)
    thinker = expert_layer(state, norm_gain, router, expert_ids, w_gate_up, w_down)
    talk_in = jnp.dot(thinker.astype(jnp.bfloat16), talk_proj, preferred_element_type=jnp.float32)
    talker = expert_layer(talk_in, talk_gain, talk_router, talk_ids, talk_gate_up, talk_down)
    return (thinker, talker)
```

```python
import functools

import jax
import jax.numpy as jnp
from jax import lax
from jax.experimental import pallas as pl
from jax.experimental.pallas import tpu as pltpu
from jax.sharding import PartitionSpec as P

H = 32
KVH = 4
HD = 128
RB = 16
F32 = jnp.float32
BF16 = jnp.bfloat16
MESH = pl.DeviceIdType.MESH


def column_dot(x_ref, w_ref, start, width):
    return jnp.dot(x_ref[...], w_ref[:, pl.ds(start, width)], preferred_element_type=F32)


def normalise(x, gain):
    scale = lax.rsqrt(jnp.mean(x * x, axis=1, keepdims=True) + 1e-06)
    return (x * scale * gain).astype(BF16)


def own_gate(normed_ref, router_ref, ids_ref, me):
    logits = lax.dot_general(
        router_ref[...], normed_ref[...], (((1,), (1,)), ((), ())), preferred_element_type=F32
    )
    rows = logits.shape[1]
    labels = lax.broadcasted_iota(jnp.int32, logits.shape, 0)
    ids = ids_ref[...]
    hit = ids[0:1, :] == labels
    for k in range(1, ids.shape[0]):
        hit = jnp.logical_or(hit, ids[k : k + 1, :] == labels)
    sig = jnp.where(hit, jax.nn.sigmoid(logits), 0.0)
    total = jnp.sum(sig, axis=0, keepdims=True)
    own = jnp.sum(jnp.where(labels == me, sig, 0.0), axis=0, keepdims=True)
    gate = jnp.broadcast_to(own / total, (rows, rows))
    diag = lax.broadcasted_iota(jnp.int32, (rows, rows), 0) == lax.broadcasted_iota(
        jnp.int32, (rows, rows), 1
    )
    return jnp.sum(jnp.where(diag, gate, 0.0), axis=1, keepdims=True)


def kernel(
    nseq,
    nexp,
    q_hbm, nkv_hbm, kv_hbm, len_ref, wo_hbm, hid_hbm, g1_hbm, rt1_hbm, id1_hbm, gu1_hbm, dn1_hbm,
    tp_hbm, g2_hbm, rt2_hbm, id2_hbm, gu2_hbm, dn2_hbm,
    out1_ref, out2_ref,
    q, nkv, kbuf, vbuf, wo, hid, g1, rt1, id1, gu1, dn1, tp, g2, rt2, id2, gu2, dn2,
    q_stage, o_stage, l_stage, att_send, att_recv, att_stage,
    head_send, head_recv, state_tile, state_send, state_all, xn1, inner1, rep1, got1,
    thk_send, thk_all, thk_bf, talk_tiles, xn2, inner2, rep2, got2, fin_send, fin_recv,
    load_sem, kv_sem, send_sem, recv_sem,
):
    ndev = nseq * nexp
    s_me = lax.axis_index("seq")
    e_me = lax.axis_index("exp")
    me = s_me * nexp + e_me
    count = kbuf.shape[0]
    span = kbuf.shape[1]
    kw = kbuf.shape[2]
    d = wo.shape[1]
    dt = tp.shape[1]
    ff = dn1.shape[0]
    ft = dn2.shape[0]
    rows = nexp * count
    nrb = rows // RB
    eb = RB // count
    hp = H // nseq
    nct1, nct2 = d // 128, dt // 128
    nt1, nt2 = nrb * nct1, nrb * nct2
    stride1, stride2 = ndev // nt1, ndev // nt2

    loads = {}

    def load(name, src, dst):
        loads[name] = pltpu.make_async_copy(src, dst, load_sem.at[len(loads)])
        loads[name].start()

    load("q", q_hbm, q)
    load("nkv", nkv_hbm, nkv)
    kv_loads = []
    for c in range(count):
        pair = [
            pltpu.make_async_copy(kv_hbm.at[0, c], kbuf.at[c], kv_sem.at[2 * c]),
            pltpu.make_async_copy(kv_hbm.at[1, c], vbuf.at[c], kv_sem.at[2 * c + 1]),
        ]
        for copy in pair:
            copy.start()
        kv_loads.append(pair)
    load("wo", wo_hbm, wo)
    load("hid", hid_hbm, hid)
    load("g1", g1_hbm, g1)
    load("rt1", rt1_hbm, rt1)
    load("id1", id1_hbm, id1)
    load("gu1", gu1_hbm.at[0], gu1)
    load("dn1", dn1_hbm.at[0], dn1)
    load("tp", tp_hbm, tp)
    load("g2", g2_hbm, g2)
    load("rt2", rt2_hbm, rt2)
    load("id2", id2_hbm, id2)
    load("gu2", gu2_hbm.at[0], gu2)
    load("dn2", dn2_hbm.at[0], dn2)

    barrier = pltpu.get_barrier_semaphore()

    def greet(k, carry):
        dev = lax.rem(me + k, ndev)
        pl.semaphore_signal(barrier, inc=1, device_id=(dev // nexp, lax.rem(dev, nexp)), device_id_type=MESH)
        return carry

    lax.fori_loop(1, ndev, greet, 0)

    def remote(src, dst, phase, dev):
        return pltpu.make_async_remote_copy(
            src_ref=src,
            dst_ref=dst,
            send_sem=send_sem.at[phase],
            recv_sem=recv_sem.at[phase],
            device_id=(dev // nexp, lax.rem(dev, nexp)),
            device_id_type=MESH,
        )

    def send(src, dst, phase, dev):
        @pl.when(dev == me)
        def _():
            pltpu.make_async_copy(src, dst, recv_sem.at[phase]).start()

        @pl.when(dev != me)
        def _():
            remote(src, dst, phase, dev).start()

    def await_bytes(ref, sem):
        pltpu.make_async_copy(ref, ref, sem).wait()

    loads["q"].wait()
    loads["nkv"].wait()
    queries = q[...].astype(F32)
    for h in range(H):
        q_stage[h * 8 : h * 8 + count, :] = queries[:, h * HD : (h + 1) * HD]
    groups = H // KVH
    head_group = lax.broadcasted_iota(jnp.int32, (H, HD), 0) // groups
    places = s_me * span + lax.broadcasted_iota(jnp.int32, (1, span), 1)
    owner = s_me == 0
    scale = HD ** (-0.5)
    for c in range(count):
        q_c = q_stage[pl.ds(c, H, stride=8), :]
        spread = jnp.concatenate(
            [jnp.where(head_group == g, q_c, 0.0) for g in range(KVH)], axis=1
        )
        new_k = nkv[0, c : c + 1, :].astype(F32)
        new_v = nkv[1, c : c + 1, :].astype(F32)
        kv_loads[c][0].wait()
        scores = lax.dot_general(
            spread.astype(BF16), kbuf[c], (((1,), (1,)), ((), ())), preferred_element_type=F32
        ) * scale
        fresh = jnp.sum(spread * new_k, axis=1, keepdims=True) * scale
        fresh = jnp.where(owner, fresh, -1e30)
        valid = places < len_ref[c]
        masked = jnp.where(valid, scores, -1e30)
        peak = jnp.maximum(jnp.max(masked, axis=1, keepdims=True), fresh)
        weights = jnp.where(valid, jnp.exp(masked - peak), 0.0).astype(BF16)
        fresh_weight = jnp.where(owner, jnp.exp(fresh - peak), 0.0)
        total = jnp.sum(weights.astype(F32), axis=1, keepdims=True) + fresh_weight
        kv_loads[c][1].wait()
        mixed = jnp.dot(weights, vbuf[c], preferred_element_type=F32) + fresh_weight * new_v
        some = total > 0.0
        safe = jnp.where(some, total, 1.0)
        lse = jnp.where(some, peak + jnp.log(safe), -1e30)
        inverse = 1.0 / safe
        mixed = mixed * inverse
        lse = jnp.broadcast_to(lse, (H, HD))
        own = mixed[:, 0:HD]
        for g in range(1, KVH):
            own = jnp.where(head_group == g, mixed[:, g * HD : (g + 1) * HD], own)
        for t in range(nseq):
            o_stage[t, c * hp : (c + 1) * hp, :] = own[t * hp : (t + 1) * hp]
            l_stage[t, c * hp : (c + 1) * hp, :] = lse[t * hp : (t + 1) * hp]

    ar = count * hp
    diag = lax.broadcasted_iota(jnp.int32, (ar, HD), 0) == lax.broadcasted_iota(jnp.int32, (ar, HD), 1)
    part_row = lax.broadcasted_iota(jnp.int32, (RB, HD), 0)
    for t in range(nseq):
        att_send[t, 0:ar, :] = o_stage[t].astype(BF16)
        line = jnp.sum(jnp.where(diag, l_stage[t], 0.0), axis=0, keepdims=True)
        high = line.astype(BF16).astype(F32)
        mid = (line - high).astype(BF16).astype(F32)
        low = line - high - mid
        parts = jnp.where(part_row == 0, high, jnp.where(part_row == 1, mid, jnp.where(part_row == 2, low, 0.0)))
        att_send[t, ar : ar + RB, :] = parts.astype(BF16)
    pl.semaphore_wait(barrier, ndev - 1)
    for k in range(nseq):
        t = lax.rem(s_me + k, nseq)
        src, dst = att_send.at[t], att_recv.at[s_me]
        if k == 0:
            pltpu.make_async_copy(src, dst, recv_sem.at[0]).start()
        else:
            remote(src, dst, 0, t * nexp + e_me).start()
    await_bytes(att_recv, recv_sem.at[0])
    lses = []
    for t in range(nseq):
        parts = att_recv[t, ar : ar + RB, :].astype(F32)
        line = parts[0:1] + parts[1:2] + parts[2:3]
        lses.append(jnp.sum(jnp.where(diag, line, 0.0), axis=1, keepdims=True))
    top = functools.reduce(jnp.maximum, lses)
    shares = [jnp.exp(x - top) for x in lses]
    norm = 1.0 / functools.reduce(jnp.add, shares)
    attn = functools.reduce(
        jnp.add, [att_recv[t, 0:ar, :].astype(F32) * (shares[t] * norm) for t in range(nseq)]
    )
    att_stage[...] = attn
    heads = jnp.concatenate(
        [att_stage[pl.ds(j, count, stride=hp), :] for j in range(hp)], axis=1
    ).astype(BF16)

    loads["wo"].wait()
    loads["hid"].wait()
    wide = 512
    for i in range(d // wide):
        at = i * wide
        term = jnp.dot(heads, wo[:, at : at + wide], preferred_element_type=F32)
        term = term + jnp.where(owner, hid[:, at : at + wide], 0.0)
        for j in range(wide // 128):
            head_send[at // 128 + j] = term[:, j * 128 : (j + 1) * 128]
    my_block = e_me // eb

    def send_terms(k, carry):
        ct = lax.rem(e_me * 2 + s_me + k, nct1)
        dev = (my_block * nct1 + ct) * stride1
        send(head_send.at[ct], head_recv.at[s_me * eb + lax.rem(e_me, eb)], 1, dev)
        return carry

    lax.fori_loop(0, nct1, send_terms, 0)
    tile1 = me // stride1
    owns1 = jnp.logical_and(lax.rem(me, stride1) == 0, tile1 < nt1)

    def send_state(k, carry):
        dev = lax.rem(me + k, ndev)
        remote(state_send, state_all.at[tile1], 2, dev).start()
        return carry

    @pl.when(owns1)
    def _():
        await_bytes(head_recv, recv_sem.at[1])
        for b in range(eb):
            state_tile[b * count : (b + 1) * count, :] = functools.reduce(
                jnp.add, [head_recv[t * eb + b] for t in range(nseq)]
            )
        state_send[...] = state_tile[...].astype(BF16)
        pltpu.make_async_copy(state_send, state_all.at[tile1], recv_sem.at[2]).start()
        lax.fori_loop(1, ndev, send_state, 0)

    def assemble(tiles, nct):
        return jnp.concatenate(
            [
                jnp.concatenate([tiles[b * nct + c].astype(F32) for c in range(nct)], axis=1)
                for b in range(nrb)
            ],
            axis=0,
        )

    def experts(xn, router, ids, gu, dn, inner, rep, width, hidden, nct):
        gate = own_gate(xn, router, ids, me)
        step = 256 if hidden % 256 == 0 else 128
        for i in range(hidden // step):
            a = column_dot(xn, gu, i * step, step)
            b = column_dot(xn, gu, hidden + i * step, step)
            inner[:, i * step : (i + 1) * step] = (a * jax.nn.sigmoid(a) * b).astype(BF16)
        for i in range(width // 256):
            y = column_dot(inner, dn, i * 256, 256).astype(BF16).astype(F32)
            y = jnp.where(gate > 0.0, gate * y, 0.0).astype(BF16)
            for r in range(nrb):
                for j in range(2):
                    rep[r * nct + i * 2 + j] = y[r * RB : (r + 1) * RB, j * 128 : (j + 1) * 128]

    def scatter(rep, got, nt, stride, phase):
        def one(k, carry):
            t = lax.rem(me // stride + k, nt)
            send(rep.at[t], got.at[me], phase, t * stride)
            return carry

        lax.fori_loop(0, nt, one, 0)

    def gather_sum(got):
        return functools.reduce(jnp.add, [got[i].astype(F32) for i in range(ndev)])

    loads["g1"].wait()
    loads["rt1"].wait()
    loads["id1"].wait()
    await_bytes(state_all, recv_sem.at[2])
    xn1[...] = normalise(assemble(state_all, nct1), g1[...])
    loads["gu1"].wait()
    loads["dn1"].wait()
    experts(xn1, rt1, id1, gu1, dn1, inner1, rep1, d, ff, nct1)
    scatter(rep1, got1, nt1, stride1, 3)

    def send_thinker(k, carry):
        dev = lax.rem(me + k, ndev)
        remote(thk_send, thk_all.at[tile1], 4, dev).start()
        return carry

    @pl.when(owns1)
    def _():
        await_bytes(got1, recv_sem.at[3])
        thk_send[...] = (state_tile[...] + gather_sum(got1)).astype(BF16)
        pltpu.make_async_copy(thk_send, thk_all.at[tile1], recv_sem.at[4]).start()
        lax.fori_loop(1, ndev, send_thinker, 0)

    loads["tp"].wait()
    loads["g2"].wait()
    loads["rt2"].wait()
    loads["id2"].wait()
    await_bytes(thk_all, recv_sem.at[4])
    thinker = assemble(thk_all, nct1)
    thk_bf[...] = thinker.astype(BF16)
    talk_parts = []
    for i in range(dt // 256):
        y = column_dot(thk_bf, tp, i * 256, 256)
        talk_parts.append(y)
        for r in range(nrb):
            for j in range(2):
                talk_tiles[r * nct2 + i * 2 + j] = y[r * RB : (r + 1) * RB, j * 128 : (j + 1) * 128]
    xn2[...] = normalise(jnp.concatenate(talk_parts, axis=1), g2[...])
    loads["gu2"].wait()
    loads["dn2"].wait()
    experts(xn2, rt2, id2, gu2, dn2, inner2, rep2, dt, ft, nct2)
    scatter(rep2, got2, nt2, stride2, 5)

    block = e_me // eb
    place = lax.rem(e_me, eb)
    mine = jnp.zeros((count, d), F32)
    for b in range(nrb):
        for k in range(eb):
            at = b * RB + k * count
            here = jnp.logical_and(block == b, place == k)
            mine = jnp.where(here, thinker[at : at + count], mine)
    out1_ref[...] = mine

    tile2 = me // stride2
    owns2 = jnp.logical_and(lax.rem(me, stride2) == 0, tile2 < nt2)
    block2, column2 = tile2 // nct2, lax.rem(tile2, nct2)

    def send_final(k, carry):
        to = lax.rem(me + k, nseq * eb)
        seq_to, at = to // eb, lax.rem(to, eb)
        send(fin_send.at[at], fin_recv.at[column2], 6, seq_to * nexp + block2 * eb + at)
        return carry

    @pl.when(owns2)
    def _():
        await_bytes(got2, recv_sem.at[5])
        tile = talk_tiles[tile2] + gather_sum(got2)
        for b in range(eb):
            fin_send[b] = tile[b * count : (b + 1) * count]
        lax.fori_loop(0, nseq * eb, send_final, 0)

    await_bytes(att_send.at[pl.ds(0, nseq - 1)], send_sem.at[0])
    for phase, sent, total, inside in (
        (1, head_send, nct1, jnp.logical_and(owns1, tile1 // nct1 == my_block)),
        (3, rep1, nt1, owns1),
        (5, rep2, nt2, owns2),
    ):

        @pl.when(inside)
        def _():
            await_bytes(sent.at[pl.ds(0, total - 1)], send_sem.at[phase])

        @pl.when(jnp.logical_not(inside))
        def _():
            await_bytes(sent.at[pl.ds(0, total)], send_sem.at[phase])

    @pl.when(owns1)
    def _():
        await_bytes(got1.at[pl.ds(0, ndev - 1)], send_sem.at[2])
        await_bytes(got1.at[pl.ds(0, ndev - 1)], send_sem.at[4])

    @pl.when(owns2)
    def _():
        @pl.when(e_me // eb == block2)
        def _():
            await_bytes(head_recv.at[pl.ds(0, nseq * eb - 1)], send_sem.at[6])

        @pl.when(e_me // eb != block2)
        def _():
            await_bytes(head_recv, send_sem.at[6])

    await_bytes(fin_recv, recv_sem.at[6])
    for j in range(nct2):
        out2_ref[:, j * 128 : (j + 1) * 128] = fin_recv[j]


def on_device(
    queries, new_kv, kv_cache, lengths, out_proj, hidden_in, norm_gain, router, expert_ids,
    w_gate_up, w_down, talk_proj, talk_gain, talk_router, talk_ids, talk_gate_up, talk_down,
):
    nseq, nexp = lax.axis_size("seq"), lax.axis_size("exp")
    ndev = nseq * nexp
    count = queries.shape[0]
    span, kw = kv_cache.shape[2:]
    d, dt = talk_proj.shape
    ff, ft = w_down.shape[1], talk_down.shape[1]
    rows = nexp * count
    nrb = rows // RB
    eb = RB // count
    hp = H // nseq
    nct1, nct2 = d // 128, dt // 128
    nt1, nt2 = nrb * nct1, nrb * nct2
    ar = count * hp
    any_spec = pl.BlockSpec(memory_space=pl.ANY)
    vmem_spec = pl.BlockSpec(memory_space=pltpu.VMEM)
    args = (
        queries, new_kv, kv_cache, lengths, out_proj, hidden_in, norm_gain.reshape(1, d), router.T,
        expert_ids.T, w_gate_up, w_down, talk_proj, talk_gain.reshape(1, dt), talk_router.T,
        talk_ids.T, talk_gate_up, talk_down,
    )
    in_specs = [any_spec] * len(args)
    in_specs[3] = pl.BlockSpec(memory_space=pltpu.SMEM)
    own = lambda x, drop=0: pltpu.VMEM(x.shape[drop:], x.dtype)
    scratch = [
        own(args[0]), own(args[1]),
        pltpu.VMEM((count, span, kw), BF16), pltpu.VMEM((count, span, kw), BF16),
        own(args[4]), own(args[5]), own(args[6]), own(args[7]), own(args[8]),
        own(args[9], 1), own(args[10], 1), own(args[11]), own(args[12]), own(args[13]), own(args[14]),
        own(args[15], 1), own(args[16], 1),
        pltpu.VMEM((H * 8, HD), F32),
        pltpu.VMEM((nseq, ar, HD), F32), pltpu.VMEM((nseq, ar, HD), F32),
        pltpu.VMEM((nseq, ar + RB, HD), BF16), pltpu.VMEM((nseq, ar + RB, HD), BF16),
        pltpu.VMEM((ar, HD), F32),
        pltpu.VMEM((nct1, count, 128), F32), pltpu.VMEM((nseq * eb, count, 128), F32),
        pltpu.VMEM((RB, 128), F32), pltpu.VMEM((RB, 128), BF16),
        pltpu.VMEM((nt1, RB, 128), BF16),
        pltpu.VMEM((rows, d), BF16), pltpu.VMEM((rows, ff), BF16),
        pltpu.VMEM((nt1, RB, 128), BF16), pltpu.VMEM((ndev, RB, 128), BF16),
        pltpu.VMEM((RB, 128), BF16), pltpu.VMEM((nt1, RB, 128), BF16),
        pltpu.VMEM((rows, d), BF16),
        pltpu.VMEM((nt2, RB, 128), F32),
        pltpu.VMEM((rows, dt), BF16), pltpu.VMEM((rows, ft), BF16),
        pltpu.VMEM((nt2, RB, 128), BF16), pltpu.VMEM((ndev, RB, 128), BF16),
        pltpu.VMEM((eb, count, 128), F32), pltpu.VMEM((nct2, count, 128), F32),
        pltpu.SemaphoreType.DMA((16,)),
        pltpu.SemaphoreType.DMA((2 * count,)),
        pltpu.SemaphoreType.DMA((7,)),
        pltpu.SemaphoreType.DMA((7,)),
    ]
    return pl.pallas_call(
        functools.partial(kernel, nseq, nexp),
        out_shape=(
            jax.ShapeDtypeStruct((count, d), F32),
            jax.ShapeDtypeStruct((count, dt), F32),
        ),
        in_specs=in_specs,
        out_specs=(vmem_spec, vmem_spec),
        scratch_shapes=scratch,
        compiler_params=pltpu.CompilerParams(
            collective_id=0, has_side_effects=True, vmem_limit_bytes=56 * 1024 * 1024
        ),
    )(*args)


def solution(mesh):
    placed = (
        P("exp", None),
        P(None, "exp", None),
        P(None, "exp", "seq", None),
        P("exp"),
        P("seq", None),
        P("exp", None),
        P(),
        P(),
        P(),
        P(("seq", "exp"), None, None),
        P(("seq", "exp"), None, None),
        P(),
        P(),
        P(),
        P(),
        P(("seq", "exp"), None, None),
        P(("seq", "exp"), None, None),
    )
    return jax.shard_map(
        on_device,
        mesh=mesh,
        in_specs=placed,
        out_specs=(P("exp", None), P("exp", None)),
        check_vma=False,
    )
```

```python
import functools

import jax
import jax.numpy as jnp
from jax import lax
from jax.experimental import pallas as pl
from jax.experimental.pallas import tpu as pltpu
from jax.sharding import PartitionSpec as P

H = 32
KVH = 4
HD = 128
RB = 16
F32 = jnp.float32
BF16 = jnp.bfloat16
MESH = pl.DeviceIdType.MESH


def column_dot(x_ref, w_ref, start, width):
    return jnp.dot(x_ref[...], w_ref[:, pl.ds(start, width)], preferred_element_type=F32)


def normalise(x, gain):
    scale = lax.rsqrt(jnp.mean(x * x, axis=1, keepdims=True) + 1e-06)
    return (x * scale * gain).astype(BF16)


def own_gate(normed_ref, router_ref, ids_ref, me):
    logits = lax.dot_general(
        router_ref[...], normed_ref[...], (((1,), (1,)), ((), ())), preferred_element_type=F32
    )
    rows = logits.shape[1]
    labels = lax.broadcasted_iota(jnp.int32, logits.shape, 0)
    ids = ids_ref[...]
    hit = ids[0:1, :] == labels
    for k in range(1, ids.shape[0]):
        hit = jnp.logical_or(hit, ids[k : k + 1, :] == labels)
    sig = jnp.where(hit, jax.nn.sigmoid(logits), 0.0)
    total = jnp.sum(sig, axis=0, keepdims=True)
    own = jnp.sum(jnp.where(labels == me, sig, 0.0), axis=0, keepdims=True)
    gate = jnp.broadcast_to(own / total, (rows, rows))
    diag = lax.broadcasted_iota(jnp.int32, (rows, rows), 0) == lax.broadcasted_iota(
        jnp.int32, (rows, rows), 1
    )
    return jnp.sum(jnp.where(diag, gate, 0.0), axis=1, keepdims=True)


def kernel(
    nseq,
    nexp,
    q_hbm, nkv_hbm, kv_hbm, len_ref, wo_hbm, hid_hbm, g1_hbm, rt1_hbm, id1_hbm, gu1_hbm, dn1_hbm,
    tp_hbm, g2_hbm, rt2_hbm, id2_hbm, gu2_hbm, dn2_hbm,
    out1_ref, out2_ref,
    q, nkv, kbuf, vbuf, wo, hid, g1, rt1, id1, gu1, dn1, tp, g2, rt2, id2, gu2, dn2,
    q_stage, o_stage, l_stage, att_send, att_recv, att_stage,
    terms, state_all, xn1, inner1, rep1, got1, part1, talk_all, xn2, inner2, rep2, got2, part2,
    load_sem, kv_sem, send_sem, recv_sem,
):
    s_me = lax.axis_index("seq")
    e_me = lax.axis_index("exp")
    me = s_me * nexp + e_me
    count = kbuf.shape[0]
    span = kbuf.shape[1]
    kw = kbuf.shape[2]
    d = wo.shape[1]
    dt = tp.shape[1]
    ff = dn1.shape[0]
    ft = dn2.shape[0]
    hp = H // nseq
    stack = RB // count

    loads = {}

    def load(name, src, dst):
        loads[name] = pltpu.make_async_copy(src, dst, load_sem.at[len(loads)])
        loads[name].start()

    load("q", q_hbm, q)
    load("nkv", nkv_hbm, nkv)
    kv_loads = []
    for c in range(count):
        pair = [
            pltpu.make_async_copy(kv_hbm.at[0, c], kbuf.at[c], kv_sem.at[2 * c]),
            pltpu.make_async_copy(kv_hbm.at[1, c], vbuf.at[c], kv_sem.at[2 * c + 1]),
        ]
        for copy in pair:
            copy.start()
        kv_loads.append(pair)
    load("wo", wo_hbm, wo)
    load("hid", hid_hbm, hid)
    load("g1", g1_hbm, g1)
    load("rt1", rt1_hbm, rt1)
    load("id1", id1_hbm, id1)
    load("gu1", gu1_hbm.at[0], gu1)
    load("dn1", dn1_hbm.at[0], dn1)
    load("tp", tp_hbm, tp)
    load("g2", g2_hbm, g2)
    load("rt2", rt2_hbm, rt2)
    load("id2", id2_hbm, id2)
    load("gu2", gu2_hbm.at[0], gu2)
    load("dn2", dn2_hbm.at[0], dn2)

    barrier = pltpu.get_barrier_semaphore()

    def along_seq(k):
        return (lax.rem(s_me + k, nseq), e_me)

    def along_exp(k):
        return (s_me, lax.rem(e_me + k, nexp))

    partners = [along_seq(k) for k in range(1, nseq)] + [along_exp(k) for k in range(1, nexp)]
    for dev in partners:
        pl.semaphore_signal(barrier, inc=1, device_id=dev, device_id_type=MESH)

    def remote(src, dst, phase, dev):
        return pltpu.make_async_remote_copy(
            src_ref=src,
            dst_ref=dst,
            send_sem=send_sem.at[phase],
            recv_sem=recv_sem.at[phase],
            device_id=dev,
            device_id_type=MESH,
        )

    def await_bytes(ref, sem):
        pltpu.make_async_copy(ref, ref, sem).wait()

    def gather(buf, phase, me_at, along, ways):
        for k in range(1, ways):
            remote(buf.at[me_at], buf.at[me_at], phase, along(k)).start()
        await_bytes(buf.at[pl.ds(0, ways - 1)], recv_sem.at[phase])

    def scatter(src, dst, phase, me_at, along, ways, axis):
        for k in range(1, ways):
            dev = along(k)
            remote(src.at[dev[axis]], dst.at[me_at], phase, dev).start()
        dst[me_at] = src[me_at]
        await_bytes(dst.at[pl.ds(0, ways - 1)], recv_sem.at[phase])

    def pack(x):
        return [
            jnp.concatenate(
                [x[:, (i * stack + k) * 128 : (i * stack + k + 1) * 128] for k in range(stack)], axis=0
            ).astype(BF16)
            for i in range(x.shape[1] // (128 * stack))
        ]

    def unpack(tiles):
        return jnp.concatenate(
            [t[k * count : (k + 1) * count] for t in tiles for k in range(stack)], axis=1
        )

    def summed(buf, ways):
        return [
            functools.reduce(jnp.add, [buf[w, i].astype(F32) for w in range(ways)])
            for i in range(buf.shape[1])
        ]

    def all_rows(buf, out):
        for i in range(buf.shape[1]):
            tiles = [buf[e, i].astype(F32) for e in range(nexp)]
            for k in range(stack):
                at = (i * stack + k) * 128
                out[:, at : at + 128] = jnp.concatenate(
                    [t[k * count : (k + 1) * count] for t in tiles], axis=0
                ).astype(BF16)

    loads["q"].wait()
    loads["nkv"].wait()
    queries = q[...].astype(F32)
    for h in range(H):
        q_stage[h * 8 : h * 8 + count, :] = queries[:, h * HD : (h + 1) * HD]
    groups = H // KVH
    head_group = lax.broadcasted_iota(jnp.int32, (H, HD), 0) // groups
    places = s_me * span + lax.broadcasted_iota(jnp.int32, (1, span), 1)
    owner = s_me == 0
    scale = HD ** (-0.5)
    for c in range(count):
        q_c = q_stage[pl.ds(c, H, stride=8), :]
        spread = jnp.concatenate(
            [jnp.where(head_group == g, q_c, 0.0) for g in range(KVH)], axis=1
        )
        new_k = nkv[0, c : c + 1, :].astype(F32)
        new_v = nkv[1, c : c + 1, :].astype(F32)
        kv_loads[c][0].wait()
        scores = lax.dot_general(
            spread.astype(BF16), kbuf[c], (((1,), (1,)), ((), ())), preferred_element_type=F32
        ) * scale
        fresh = jnp.sum(spread * new_k, axis=1, keepdims=True) * scale
        fresh = jnp.where(owner, fresh, -1e30)
        valid = places < len_ref[c]
        masked = jnp.where(valid, scores, -1e30)
        peak = jnp.maximum(jnp.max(masked, axis=1, keepdims=True), fresh)
        weights = jnp.where(valid, jnp.exp(masked - peak), 0.0).astype(BF16)
        fresh_weight = jnp.where(owner, jnp.exp(fresh - peak), 0.0)
        total = jnp.sum(weights.astype(F32), axis=1, keepdims=True) + fresh_weight
        kv_loads[c][1].wait()
        mixed = jnp.dot(weights, vbuf[c], preferred_element_type=F32) + fresh_weight * new_v
        some = total > 0.0
        safe = jnp.where(some, total, 1.0)
        lse = jnp.where(some, peak + jnp.log(safe), -1e30)
        inverse = 1.0 / safe
        mixed = mixed * inverse
        lse = jnp.broadcast_to(lse, (H, HD))
        own = mixed[:, 0:HD]
        for g in range(1, KVH):
            own = jnp.where(head_group == g, mixed[:, g * HD : (g + 1) * HD], own)
        for t in range(nseq):
            o_stage[t, c * hp : (c + 1) * hp, :] = own[t * hp : (t + 1) * hp]
            l_stage[t, c * hp : (c + 1) * hp, :] = lse[t * hp : (t + 1) * hp]

    ar = count * hp
    diag = lax.broadcasted_iota(jnp.int32, (ar, HD), 0) == lax.broadcasted_iota(jnp.int32, (ar, HD), 1)
    part_row = lax.broadcasted_iota(jnp.int32, (RB, HD), 0)
    for t in range(nseq):
        att_send[t, 0:ar, :] = o_stage[t].astype(BF16)
        line = jnp.sum(jnp.where(diag, l_stage[t], 0.0), axis=0, keepdims=True)
        high = line.astype(BF16).astype(F32)
        mid = (line - high).astype(BF16).astype(F32)
        low = line - high - mid
        parts = jnp.where(part_row == 0, high, jnp.where(part_row == 1, mid, jnp.where(part_row == 2, low, 0.0)))
        att_send[t, ar : ar + RB, :] = parts.astype(BF16)
    pl.semaphore_wait(barrier, nseq + nexp - 2)
    scatter(att_send, att_recv, 0, s_me, along_seq, nseq, 0)
    lses = []
    for t in range(nseq):
        parts = att_recv[t, ar : ar + RB, :].astype(F32)
        line = parts[0:1] + parts[1:2] + parts[2:3]
        lses.append(jnp.sum(jnp.where(diag, line, 0.0), axis=1, keepdims=True))
    top = functools.reduce(jnp.maximum, lses)
    shares = [jnp.exp(x - top) for x in lses]
    norm = 1.0 / functools.reduce(jnp.add, shares)
    attn = functools.reduce(
        jnp.add, [att_recv[t, 0:ar, :].astype(F32) * (shares[t] * norm) for t in range(nseq)]
    )
    att_stage[...] = attn
    heads = jnp.concatenate(
        [att_stage[pl.ds(j, count, stride=hp), :] for j in range(hp)], axis=1
    ).astype(BF16)

    loads["wo"].wait()
    wide = 128 * stack
    for i in range(d // wide):
        term = jnp.dot(heads, wo[:, i * wide : (i + 1) * wide], preferred_element_type=F32)
        terms[s_me, i] = pack(term)[0]
    gather(terms, 1, s_me, along_seq, nseq)
    loads["hid"].wait()
    loads["g1"].wait()
    state = hid[...] + unpack(summed(terms, nseq))

    def experts(xn, router, ids, gu, dn, inner, rep, width, hidden):
        gate = own_gate(xn, router, ids, me)
        step = 256 if hidden % 256 == 0 else 128
        for i in range(hidden // step):
            a = column_dot(xn, gu, i * step, step)
            b = column_dot(xn, gu, hidden + i * step, step)
            inner[:, i * step : (i + 1) * step] = (a * jax.nn.sigmoid(a) * b).astype(BF16)
        for i in range(width // wide):
            y = column_dot(inner, dn, i * wide, wide).astype(BF16).astype(F32)
            y = jnp.where(gate > 0.0, gate * y, 0.0)
            for e in range(nexp):
                rep[e, i] = pack(y[e * count : (e + 1) * count])[0]

    def layer(stream, gain, everyone, xn, router, ids, gu, dn, inner, rep, got, part, phase, names):
        for i, tile in enumerate(pack(normalise(stream, gain).astype(F32))):
            everyone[e_me, i] = tile
        gather(everyone, phase, e_me, along_exp, nexp)
        all_rows(everyone, xn)
        for name in names:
            loads[name].wait()
        experts(xn, router, ids, gu, dn, inner, rep, stream.shape[1], inner.shape[1])
        scatter(rep, got, phase + 1, e_me, along_exp, nexp, 1)
        for i, tile in enumerate(summed(got, nexp)):
            part[s_me, i] = tile.astype(BF16)
        gather(part, phase + 2, s_me, along_seq, nseq)
        return stream + unpack(summed(part, nseq))

    thinker = layer(
        state, g1[...], state_all, xn1, rt1, id1, gu1, dn1, inner1, rep1, got1, part1, 2,
        ("rt1", "id1", "gu1", "dn1"),
    )
    out1_ref[...] = thinker
    loads["tp"].wait()
    loads["g2"].wait()
    thinker_bf = thinker.astype(BF16)
    talk_in = jnp.concatenate(
        [
            jnp.dot(thinker_bf, tp[:, i * wide : (i + 1) * wide], preferred_element_type=F32)
            for i in range(dt // wide)
        ],
        axis=1,
    )
    out2_ref[...] = layer(
        talk_in, g2[...], talk_all, xn2, rt2, id2, gu2, dn2, inner2, rep2, got2, part2, 5,
        ("rt2", "id2", "gu2", "dn2"),
    )

    for phase, buf, ways in (
        (0, att_send, nseq),
        (1, terms, nseq),
        (2, state_all, nexp),
        (3, rep1, nexp),
        (4, part1, nseq),
        (5, talk_all, nexp),
        (6, rep2, nexp),
        (7, part2, nseq),
    ):
        await_bytes(buf.at[pl.ds(0, ways - 1)], send_sem.at[phase])


def on_device(
    queries, new_kv, kv_cache, lengths, out_proj, hidden_in, norm_gain, router, expert_ids,
    w_gate_up, w_down, talk_proj, talk_gain, talk_router, talk_ids, talk_gate_up, talk_down,
):
    nseq, nexp = lax.axis_size("seq"), lax.axis_size("exp")
    count = queries.shape[0]
    span, kw = kv_cache.shape[2:]
    d, dt = talk_proj.shape
    ff, ft = w_down.shape[1], talk_down.shape[1]
    rows = nexp * count
    hp = H // nseq
    ar = count * hp
    wide = 128 * (RB // count)
    any_spec = pl.BlockSpec(memory_space=pl.ANY)
    vmem_spec = pl.BlockSpec(memory_space=pltpu.VMEM)
    args = (
        queries, new_kv, kv_cache, lengths, out_proj, hidden_in, norm_gain.reshape(1, d), router.T,
        expert_ids.T, w_gate_up, w_down, talk_proj, talk_gain.reshape(1, dt), talk_router.T,
        talk_ids.T, talk_gate_up, talk_down,
    )
    in_specs = [any_spec] * len(args)
    in_specs[3] = pl.BlockSpec(memory_space=pltpu.SMEM)
    own = lambda x, drop=0: pltpu.VMEM(x.shape[drop:], x.dtype)
    scratch = [
        own(args[0]), own(args[1]),
        pltpu.VMEM((count, span, kw), BF16), pltpu.VMEM((count, span, kw), BF16),
        own(args[4]), own(args[5]), own(args[6]), own(args[7]), own(args[8]),
        own(args[9], 1), own(args[10], 1), own(args[11]), own(args[12]), own(args[13]), own(args[14]),
        own(args[15], 1), own(args[16], 1),
        pltpu.VMEM((H * 8, HD), F32),
        pltpu.VMEM((nseq, ar, HD), F32), pltpu.VMEM((nseq, ar, HD), F32),
        pltpu.VMEM((nseq, ar + RB, HD), BF16), pltpu.VMEM((nseq, ar + RB, HD), BF16),
        pltpu.VMEM((ar, HD), F32),
        pltpu.VMEM((nseq, d // wide, RB, 128), BF16),
        pltpu.VMEM((nexp, d // wide, RB, 128), BF16),
        pltpu.VMEM((rows, d), BF16), pltpu.VMEM((rows, ff), BF16),
        pltpu.VMEM((nexp, d // wide, RB, 128), BF16), pltpu.VMEM((nexp, d // wide, RB, 128), BF16),
        pltpu.VMEM((nseq, d // wide, RB, 128), BF16),
        pltpu.VMEM((nexp, dt // wide, RB, 128), BF16),
        pltpu.VMEM((rows, dt), BF16), pltpu.VMEM((rows, ft), BF16),
        pltpu.VMEM((nexp, dt // wide, RB, 128), BF16), pltpu.VMEM((nexp, dt // wide, RB, 128), BF16),
        pltpu.VMEM((nseq, dt // wide, RB, 128), BF16),
        pltpu.SemaphoreType.DMA((16,)),
        pltpu.SemaphoreType.DMA((2 * count,)),
        pltpu.SemaphoreType.DMA((8,)),
        pltpu.SemaphoreType.DMA((8,)),
    ]
    return pl.pallas_call(
        functools.partial(kernel, nseq, nexp),
        out_shape=(
            jax.ShapeDtypeStruct((count, d), F32),
            jax.ShapeDtypeStruct((count, dt), F32),
        ),
        in_specs=in_specs,
        out_specs=(vmem_spec, vmem_spec),
        scratch_shapes=scratch,
        compiler_params=pltpu.CompilerParams(
            collective_id=0, has_side_effects=True, vmem_limit_bytes=56 * 1024 * 1024
        ),
    )(*args)


def solution(mesh):
    placed = (
        P("exp", None),
        P(None, "exp", None),
        P(None, "exp", "seq", None),
        P("exp"),
        P("seq", None),
        P("exp", None),
        P(),
        P(),
        P(),
        P(("seq", "exp"), None, None),
        P(("seq", "exp"), None, None),
        P(),
        P(),
        P(),
        P(),
        P(("seq", "exp"), None, None),
        P(("seq", "exp"), None, None),
    )
    return jax.shard_map(
        on_device,
        mesh=mesh,
        in_specs=placed,
        out_specs=(P("exp", None), P("exp", None)),
        check_vma=False,
    )
```

```python
import functools

import jax
import jax.numpy as jnp
from jax import lax
from jax.experimental import pallas as pl
from jax.experimental.pallas import tpu as pltpu
from jax.sharding import PartitionSpec as P

H = 32
KVH = 4
HD = 128
RB = 16
F32 = jnp.float32
BF16 = jnp.bfloat16
MESH = pl.DeviceIdType.MESH


def column_dot(x_ref, w_ref, start, width):
    return jnp.dot(x_ref[...], w_ref[:, pl.ds(start, width)], preferred_element_type=F32)


def normalise(x, gain):
    scale = lax.rsqrt(jnp.mean(x * x, axis=1, keepdims=True) + 1e-06)
    return (x * scale * gain).astype(BF16)


def own_gate(normed_ref, router_ref, ids_ref, me):
    logits = lax.dot_general(
        router_ref[...], normed_ref[...], (((1,), (1,)), ((), ())), preferred_element_type=F32
    )
    rows = logits.shape[1]
    labels = lax.broadcasted_iota(jnp.int32, logits.shape, 0)
    ids = ids_ref[...]
    hit = ids[0:1, :] == labels
    for k in range(1, ids.shape[0]):
        hit = jnp.logical_or(hit, ids[k : k + 1, :] == labels)
    sig = jnp.where(hit, jax.nn.sigmoid(logits), 0.0)
    total = jnp.sum(sig, axis=0, keepdims=True)
    own = jnp.sum(jnp.where(labels == me, sig, 0.0), axis=0, keepdims=True)
    gate = jnp.broadcast_to(own / total, (rows, rows))
    diag = lax.broadcasted_iota(jnp.int32, (rows, rows), 0) == lax.broadcasted_iota(
        jnp.int32, (rows, rows), 1
    )
    return jnp.sum(jnp.where(diag, gate, 0.0), axis=1, keepdims=True)


def kernel(
    nseq,
    nexp,
    q_hbm, nkv_hbm, kv_hbm, len_ref, wo_hbm, hid_hbm, g1_hbm, rt1_hbm, id1_hbm, gu1_hbm, dn1_hbm,
    tp_hbm, g2_hbm, rt2_hbm, id2_hbm, gu2_hbm, dn2_hbm,
    out1_ref, out2_ref,
    q, nkv, kbuf, vbuf, wo, hid, g1, rt1, id1, gu1, dn1, tp, g2, rt2, id2, gu2, dn2,
    q_stage, o_stage, l_stage, att_send, att_recv, att_stage,
    terms, state_all, xn1, inner1, rep1, got1, part1, talk_all, xn2, inner2, rep2, got2, part2,
    load_sem, send_sem, recv_sem,
):
    s_me = lax.axis_index("seq")
    e_me = lax.axis_index("exp")
    me = s_me * nexp + e_me
    count = kbuf.shape[0]
    span = kbuf.shape[1]
    kw = kbuf.shape[2]
    d = wo.shape[1]
    dt = tp.shape[1]
    ff = dn1.shape[0]
    ft = dn2.shape[0]
    hp = H // nseq
    stack = RB // count

    loads = {}

    def load(name, src, dst):
        loads[name] = pltpu.make_async_copy(src, dst, load_sem.at[len(loads)])
        loads[name].start()

    load("q", q_hbm, q)
    load("nkv", nkv_hbm, nkv)
    load("keys", kv_hbm.at[0], kbuf)
    load("values", kv_hbm.at[1], vbuf)

    barrier = pltpu.get_barrier_semaphore()

    def along_seq(k):
        return (lax.rem(s_me + k, nseq), e_me)

    def along_exp(k):
        to, bit = e_me, 1
        while bit < nexp:
            if (nexp - k) & bit:
                to = to + bit * (1 - 2 * lax.rem(e_me // bit, 2))
            bit = 2 * bit
        return (s_me, to)

    partners = [along_seq(k) for k in range(1, nseq)] + [along_exp(k) for k in range(1, nexp)]
    for dev in partners:
        pl.semaphore_signal(barrier, inc=1, device_id=dev, device_id_type=MESH)

    def remote(src, dst, phase, dev):
        return pltpu.make_async_remote_copy(
            src_ref=src,
            dst_ref=dst,
            send_sem=send_sem.at[phase],
            recv_sem=recv_sem.at[phase],
            device_id=dev,
            device_id_type=MESH,
        )

    def await_bytes(ref, sem):
        pltpu.make_async_copy(ref, ref, sem).wait()

    def gather(buf, phase, me_at, along, ways):
        for k in range(1, ways):
            remote(buf.at[me_at], buf.at[me_at], phase, along(k)).start()
        await_bytes(buf.at[pl.ds(0, ways - 1)], recv_sem.at[phase])

    def scatter(src, dst, phase, me_at, along, ways, axis):
        for k in range(1, ways):
            dev = along(k)
            remote(src.at[dev[axis]], dst.at[me_at], phase, dev).start()
        dst[me_at] = src[me_at]
        await_bytes(dst.at[pl.ds(0, ways - 1)], recv_sem.at[phase])

    def pack(x):
        return [
            jnp.concatenate(
                [x[:, (i * stack + k) * 128 : (i * stack + k + 1) * 128] for k in range(stack)], axis=0
            ).astype(BF16)
            for i in range(x.shape[1] // (128 * stack))
        ]

    def unpack(tiles):
        return jnp.concatenate(
            [t[k * count : (k + 1) * count] for t in tiles for k in range(stack)], axis=1
        )

    def summed(buf, ways):
        return [
            functools.reduce(jnp.add, [buf[w, i].astype(F32) for w in range(ways)])
            for i in range(buf.shape[1])
        ]

    def all_rows(buf, out):
        for i in range(buf.shape[1]):
            tiles = [buf[e, i].astype(F32) for e in range(nexp)]
            for k in range(stack):
                at = (i * stack + k) * 128
                out[:, at : at + 128] = jnp.concatenate(
                    [t[k * count : (k + 1) * count] for t in tiles], axis=0
                ).astype(BF16)

    loads["q"].wait()
    loads["nkv"].wait()
    queries = q[...].astype(F32)
    for h in range(H):
        q_stage[h * 8 : h * 8 + count, :] = queries[:, h * HD : (h + 1) * HD]
    groups = H // KVH
    head_group = lax.broadcasted_iota(jnp.int32, (H, HD), 0) // groups
    places = s_me * span + lax.broadcasted_iota(jnp.int32, (1, span), 1)
    owner = s_me == 0
    scale = HD ** (-0.5)
    every = range(count)
    spread = []
    for c in every:
        q_c = q_stage[pl.ds(c, H, stride=8), :]
        spread.append(
            jnp.concatenate([jnp.where(head_group == g, q_c, 0.0) for g in range(KVH)], axis=1)
        )
    fresh = [
        jnp.sum(spread[c] * nkv[0, c : c + 1, :].astype(F32), axis=1, keepdims=True) * scale
        for c in every
    ]
    fresh = [jnp.where(owner, x, -1e30) for x in fresh]
    valid = [places < len_ref[c] for c in every]
    loads["keys"].wait()
    load("wo", wo_hbm, wo)
    scores = [
        lax.dot_general(
            spread[c].astype(BF16), kbuf[c], (((1,), (1,)), ((), ())), preferred_element_type=F32
        )
        * scale
        for c in every
    ]
    masked = [jnp.where(valid[c], scores[c], -1e30) for c in every]
    peak = [jnp.maximum(jnp.max(masked[c], axis=1, keepdims=True), fresh[c]) for c in every]
    weights = [
        jnp.where(valid[c], jnp.exp(masked[c] - peak[c]), 0.0).astype(BF16) for c in every
    ]
    fresh_weight = [jnp.where(owner, jnp.exp(fresh[c] - peak[c]), 0.0) for c in every]
    total = [
        jnp.sum(weights[c].astype(F32), axis=1, keepdims=True) + fresh_weight[c] for c in every
    ]
    loads["values"].wait()
    load("hid", hid_hbm, hid)
    load("g1", g1_hbm, g1)
    load("rt1", rt1_hbm, rt1)
    load("id1", id1_hbm, id1)
    load("gu1", gu1_hbm.at[0], gu1)
    load("dn1", dn1_hbm.at[0], dn1)
    load("tp", tp_hbm, tp)
    load("g2", g2_hbm, g2)
    load("rt2", rt2_hbm, rt2)
    load("id2", id2_hbm, id2)
    load("gu2", gu2_hbm.at[0], gu2)
    load("dn2", dn2_hbm.at[0], dn2)
    mixed = [jnp.dot(weights[c], vbuf[c], preferred_element_type=F32) for c in every]
    for c in every:
        some = total[c] > 0.0
        safe = jnp.where(some, total[c], 1.0)
        lse = jnp.broadcast_to(jnp.where(some, peak[c] + jnp.log(safe), -1e30), (H, HD))
        whole = (mixed[c] + fresh_weight[c] * nkv[1, c : c + 1, :].astype(F32)) * (1.0 / safe)
        own = whole[:, 0:HD]
        for g in range(1, KVH):
            own = jnp.where(head_group == g, whole[:, g * HD : (g + 1) * HD], own)
        for t in range(nseq):
            o_stage[t, c * hp : (c + 1) * hp, :] = own[t * hp : (t + 1) * hp]
            l_stage[t, c * hp : (c + 1) * hp, :] = lse[t * hp : (t + 1) * hp]

    ar = count * hp
    diag = lax.broadcasted_iota(jnp.int32, (ar, HD), 0) == lax.broadcasted_iota(jnp.int32, (ar, HD), 1)
    part_row = lax.broadcasted_iota(jnp.int32, (RB, HD), 0)
    for t in range(nseq):
        att_send[t, 0:ar, :] = o_stage[t].astype(BF16)
        line = jnp.sum(jnp.where(diag, l_stage[t], 0.0), axis=0, keepdims=True)
        high = line.astype(BF16).astype(F32)
        mid = (line - high).astype(BF16).astype(F32)
        low = line - high - mid
        parts = jnp.where(part_row == 0, high, jnp.where(part_row == 1, mid, jnp.where(part_row == 2, low, 0.0)))
        att_send[t, ar : ar + RB, :] = parts.astype(BF16)
    pl.semaphore_wait(barrier, nseq + nexp - 2)
    scatter(att_send, att_recv, 0, s_me, along_seq, nseq, 0)
    lses = []
    for t in range(nseq):
        parts = att_recv[t, ar : ar + RB, :].astype(F32)
        line = parts[0:1] + parts[1:2] + parts[2:3]
        lses.append(jnp.sum(jnp.where(diag, line, 0.0), axis=1, keepdims=True))
    top = functools.reduce(jnp.maximum, lses)
    shares = [jnp.exp(x - top) for x in lses]
    norm = 1.0 / functools.reduce(jnp.add, shares)
    attn = functools.reduce(
        jnp.add, [att_recv[t, 0:ar, :].astype(F32) * (shares[t] * norm) for t in range(nseq)]
    )
    att_stage[...] = attn
    heads = jnp.concatenate(
        [att_stage[pl.ds(j, count, stride=hp), :] for j in range(hp)], axis=1
    ).astype(BF16)

    loads["wo"].wait()
    wide = 128 * stack
    for i in range(d // wide):
        term = jnp.dot(heads, wo[:, i * wide : (i + 1) * wide], preferred_element_type=F32)
        terms[s_me, i] = pack(term)[0]
    gather(terms, 1, s_me, along_seq, nseq)
    loads["hid"].wait()
    loads["g1"].wait()
    state = hid[...] + unpack(summed(terms, nseq))

    def experts(xn, router, ids, gu, dn, inner, rep, width, hidden):
        gate = own_gate(xn, router, ids, me)
        step = 256 if hidden % 256 == 0 else 128
        for i in range(hidden // step):
            a = column_dot(xn, gu, i * step, step)
            b = column_dot(xn, gu, hidden + i * step, step)
            inner[:, i * step : (i + 1) * step] = (a * jax.nn.sigmoid(a) * b).astype(BF16)
        for i in range(width // wide):
            y = column_dot(inner, dn, i * wide, wide).astype(BF16).astype(F32)
            y = jnp.where(gate > 0.0, gate * y, 0.0)
            for e in range(nexp):
                rep[e, i] = pack(y[e * count : (e + 1) * count])[0]

    def layer(stream, gain, everyone, xn, router, ids, gu, dn, inner, rep, got, part, phase, names):
        for i, tile in enumerate(pack(normalise(stream, gain).astype(F32))):
            everyone[e_me, i] = tile
        gather(everyone, phase, e_me, along_exp, nexp)
        all_rows(everyone, xn)
        for name in names:
            loads[name].wait()
        experts(xn, router, ids, gu, dn, inner, rep, stream.shape[1], inner.shape[1])
        scatter(rep, got, phase + 1, e_me, along_exp, nexp, 1)
        for i, tile in enumerate(summed(got, nexp)):
            part[s_me, i] = tile.astype(BF16)
        gather(part, phase + 2, s_me, along_seq, nseq)
        return stream + unpack(summed(part, nseq))

    thinker = layer(
        state, g1[...], state_all, xn1, rt1, id1, gu1, dn1, inner1, rep1, got1, part1, 2,
        ("rt1", "id1", "gu1", "dn1"),
    )
    out1_ref[...] = thinker
    loads["tp"].wait()
    loads["g2"].wait()
    thinker_bf = thinker.astype(BF16)
    talk_in = jnp.concatenate(
        [
            jnp.dot(thinker_bf, tp[:, i * wide : (i + 1) * wide], preferred_element_type=F32)
            for i in range(dt // wide)
        ],
        axis=1,
    )
    out2_ref[...] = layer(
        talk_in, g2[...], talk_all, xn2, rt2, id2, gu2, dn2, inner2, rep2, got2, part2, 5,
        ("rt2", "id2", "gu2", "dn2"),
    )

    for phase, buf, ways in (
        (0, att_send, nseq),
        (1, terms, nseq),
        (2, state_all, nexp),
        (3, rep1, nexp),
        (4, part1, nseq),
        (5, talk_all, nexp),
        (6, rep2, nexp),
        (7, part2, nseq),
    ):
        await_bytes(buf.at[pl.ds(0, ways - 1)], send_sem.at[phase])


def on_device(
    queries, new_kv, kv_cache, lengths, out_proj, hidden_in, norm_gain, router, expert_ids,
    w_gate_up, w_down, talk_proj, talk_gain, talk_router, talk_ids, talk_gate_up, talk_down,
):
    nseq, nexp = lax.axis_size("seq"), lax.axis_size("exp")
    count = queries.shape[0]
    span, kw = kv_cache.shape[2:]
    d, dt = talk_proj.shape
    ff, ft = w_down.shape[1], talk_down.shape[1]
    rows = nexp * count
    hp = H // nseq
    ar = count * hp
    wide = 128 * (RB // count)
    any_spec = pl.BlockSpec(memory_space=pl.ANY)
    vmem_spec = pl.BlockSpec(memory_space=pltpu.VMEM)
    args = (
        queries, new_kv, kv_cache, lengths, out_proj, hidden_in, norm_gain.reshape(1, d), router.T,
        expert_ids.T, w_gate_up, w_down, talk_proj, talk_gain.reshape(1, dt), talk_router.T,
        talk_ids.T, talk_gate_up, talk_down,
    )
    in_specs = [any_spec] * len(args)
    in_specs[3] = pl.BlockSpec(memory_space=pltpu.SMEM)
    own = lambda x, drop=0: pltpu.VMEM(x.shape[drop:], x.dtype)
    scratch = [
        own(args[0]), own(args[1]),
        pltpu.VMEM((count, span, kw), BF16), pltpu.VMEM((count, span, kw), BF16),
        own(args[4]), own(args[5]), own(args[6]), own(args[7]), own(args[8]),
        own(args[9], 1), own(args[10], 1), own(args[11]), own(args[12]), own(args[13]), own(args[14]),
        own(args[15], 1), own(args[16], 1),
        pltpu.VMEM((H * 8, HD), F32),
        pltpu.VMEM((nseq, ar, HD), F32), pltpu.VMEM((nseq, ar, HD), F32),
        pltpu.VMEM((nseq, ar + RB, HD), BF16), pltpu.VMEM((nseq, ar + RB, HD), BF16),
        pltpu.VMEM((ar, HD), F32),
        pltpu.VMEM((nseq, d // wide, RB, 128), BF16),
        pltpu.VMEM((nexp, d // wide, RB, 128), BF16),
        pltpu.VMEM((rows, d), BF16), pltpu.VMEM((rows, ff), BF16),
        pltpu.VMEM((nexp, d // wide, RB, 128), BF16), pltpu.VMEM((nexp, d // wide, RB, 128), BF16),
        pltpu.VMEM((nseq, d // wide, RB, 128), BF16),
        pltpu.VMEM((nexp, dt // wide, RB, 128), BF16),
        pltpu.VMEM((rows, dt), BF16), pltpu.VMEM((rows, ft), BF16),
        pltpu.VMEM((nexp, dt // wide, RB, 128), BF16), pltpu.VMEM((nexp, dt // wide, RB, 128), BF16),
        pltpu.VMEM((nseq, dt // wide, RB, 128), BF16),
        pltpu.SemaphoreType.DMA((17,)),
        pltpu.SemaphoreType.DMA((8,)),
        pltpu.SemaphoreType.DMA((8,)),
    ]
    return pl.pallas_call(
        functools.partial(kernel, nseq, nexp),
        out_shape=(
            jax.ShapeDtypeStruct((count, d), F32),
            jax.ShapeDtypeStruct((count, dt), F32),
        ),
        in_specs=in_specs,
        out_specs=(vmem_spec, vmem_spec),
        scratch_shapes=scratch,
        compiler_params=pltpu.CompilerParams(
            collective_id=0, has_side_effects=True, vmem_limit_bytes=56 * 1024 * 1024
        ),
    )(*args)


def solution(mesh):
    placed = (
        P("exp", None),
        P(None, "exp", None),
        P(None, "exp", "seq", None),
        P("exp"),
        P("seq", None),
        P("exp", None),
        P(),
        P(),
        P(),
        P(("seq", "exp"), None, None),
        P(("seq", "exp"), None, None),
        P(),
        P(),
        P(),
        P(),
        P(("seq", "exp"), None, None),
        P(("seq", "exp"), None, None),
    )
    return jax.shard_map(
        on_device,
        mesh=mesh,
        in_specs=placed,
        out_specs=(P("exp", None), P("exp", None)),
        check_vma=False,
    )
```

```python
import functools

import jax
import jax.numpy as jnp
from jax import lax
from jax.experimental import pallas as pl
from jax.experimental.pallas import tpu as pltpu
from jax.sharding import PartitionSpec as P

H = 32
KVH = 4
HD = 128
RB = 16
F32 = jnp.float32
BF16 = jnp.bfloat16
MESH = pl.DeviceIdType.MESH


def column_dot(x_ref, w_ref, start, width):
    return jnp.dot(x_ref[...], w_ref[:, pl.ds(start, width)], preferred_element_type=F32)


def normalise(x, gain):
    scale = lax.rsqrt(jnp.mean(x * x, axis=1, keepdims=True) + 1e-06)
    return (x * scale * gain).astype(BF16)


def own_gate(normed_ref, router_ref, ids_ref, me):
    logits = lax.dot_general(
        router_ref[...], normed_ref[...], (((1,), (1,)), ((), ())), preferred_element_type=F32
    )
    rows = logits.shape[1]
    labels = lax.broadcasted_iota(jnp.int32, logits.shape, 0)
    ids = ids_ref[...]
    hit = ids[0:1, :] == labels
    for k in range(1, ids.shape[0]):
        hit = jnp.logical_or(hit, ids[k : k + 1, :] == labels)
    sig = jnp.where(hit, jax.nn.sigmoid(logits), 0.0)
    total = jnp.sum(sig, axis=0, keepdims=True)
    own = jnp.sum(jnp.where(labels == me, sig, 0.0), axis=0, keepdims=True)
    gate = jnp.broadcast_to(own / total, (rows, rows))
    diag = lax.broadcasted_iota(jnp.int32, (rows, rows), 0) == lax.broadcasted_iota(
        jnp.int32, (rows, rows), 1
    )
    return jnp.sum(jnp.where(diag, gate, 0.0), axis=1, keepdims=True)


def kernel(
    nseq,
    nexp,
    q_hbm, nkv_hbm, kv_hbm, len_ref, wo_hbm, hid_hbm, g1_hbm, rt1_hbm, id1_hbm, gu1_hbm, dn1_hbm,
    tp_hbm, g2_hbm, rt2_hbm, id2_hbm, gu2_hbm, dn2_hbm,
    out1_ref, out2_ref,
    q, nkv, kbuf, vbuf, wo, hid, g1, rt1, id1, gu1, dn1, tp, g2, rt2, id2, gu2, dn2,
    q_stage, o_stage, l_stage, att_send, att_recv, att_stage,
    terms, state_all, xn1, inner1, rep1, got1, part1, talk_all, xn2, inner2, rep2, got2, part2,
    load_sem, send_sem, recv_sem,
):
    s_me = lax.axis_index("seq")
    e_me = lax.axis_index("exp")
    me = s_me * nexp + e_me
    count = kbuf.shape[0]
    span = kbuf.shape[1]
    kw = kbuf.shape[2]
    d = wo.shape[1]
    dt = tp.shape[1]
    ff = dn1.shape[0]
    ft = dn2.shape[0]
    hp = H // nseq
    stack = RB // count

    loads = {}

    def load(name, src, dst):
        loads[name] = pltpu.make_async_copy(src, dst, load_sem.at[len(loads)])
        loads[name].start()

    load("q", q_hbm, q)
    load("nkv", nkv_hbm, nkv)
    load("keys", kv_hbm.at[0], kbuf)
    load("values", kv_hbm.at[1], vbuf)

    barrier = pltpu.get_barrier_semaphore()

    def along_seq(k):
        return (lax.rem(s_me + k, nseq), e_me)

    def along_exp(k):
        to, bit = e_me, 1
        while bit < nexp:
            if (nexp - k) & bit:
                to = to + bit * (1 - 2 * lax.rem(e_me // bit, 2))
            bit = 2 * bit
        return (s_me, to)

    partners = [along_seq(k) for k in range(1, nseq)] + [along_exp(k) for k in range(1, nexp)]
    for dev in partners:
        pl.semaphore_signal(barrier, inc=1, device_id=dev, device_id_type=MESH)

    def remote(src, dst, phase, dev):
        return pltpu.make_async_remote_copy(
            src_ref=src,
            dst_ref=dst,
            send_sem=send_sem.at[phase],
            recv_sem=recv_sem.at[phase],
            device_id=dev,
            device_id_type=MESH,
        )

    def await_bytes(ref, sem):
        pltpu.make_async_copy(ref, ref, sem).wait()

    def gather(buf, phase, me_at, along, ways):
        for k in range(1, ways):
            remote(buf.at[me_at], buf.at[me_at], phase, along(k)).start()
        await_bytes(buf.at[pl.ds(0, ways - 1)], recv_sem.at[phase])

    def scatter(src, dst, phase, me_at, along, ways, axis):
        for k in range(1, ways):
            dev = along(k)
            remote(src.at[dev[axis]], dst.at[me_at], phase, dev).start()
        dst[me_at] = src[me_at]
        await_bytes(dst.at[pl.ds(0, ways - 1)], recv_sem.at[phase])

    def pack(x):
        return [
            jnp.concatenate(
                [x[:, (i * stack + k) * 128 : (i * stack + k + 1) * 128] for k in range(stack)], axis=0
            ).astype(BF16)
            for i in range(x.shape[1] // (128 * stack))
        ]

    def unpack(tiles):
        return jnp.concatenate(
            [t[k * count : (k + 1) * count] for t in tiles for k in range(stack)], axis=1
        )

    def summed(buf, ways):
        return [
            functools.reduce(jnp.add, [buf[w, i].astype(F32) for w in range(ways)])
            for i in range(buf.shape[1])
        ]

    def all_rows(buf, out):
        for i in range(buf.shape[1]):
            tiles = [buf[e, i].astype(F32) for e in range(nexp)]
            for k in range(stack):
                at = (i * stack + k) * 128
                out[:, at : at + 128] = jnp.concatenate(
                    [t[k * count : (k + 1) * count] for t in tiles], axis=0
                ).astype(BF16)

    loads["q"].wait()
    loads["nkv"].wait()
    queries = q[...].astype(F32)
    for h in range(H):
        q_stage[h * 8 : h * 8 + count, :] = queries[:, h * HD : (h + 1) * HD]
    groups = H // KVH
    head_group = lax.broadcasted_iota(jnp.int32, (H, HD), 0) // groups
    places = s_me * span + lax.broadcasted_iota(jnp.int32, (1, span), 1)
    owner = s_me == 0
    scale = HD ** (-0.5)
    every = range(count)
    spread = []
    for c in every:
        q_c = q_stage[pl.ds(c, H, stride=8), :]
        spread.append(
            jnp.concatenate([jnp.where(head_group == g, q_c, 0.0) for g in range(KVH)], axis=1)
        )
    fresh = [
        jnp.sum(spread[c] * nkv[0, c : c + 1, :].astype(F32), axis=1, keepdims=True) * scale
        for c in every
    ]
    fresh = [jnp.where(owner, x, -1e30) for x in fresh]
    valid = [places < len_ref[c] for c in every]
    loads["keys"].wait()
    load("wo", wo_hbm, wo)
    scores = [
        lax.dot_general(
            spread[c].astype(BF16), kbuf[c], (((1,), (1,)), ((), ())), preferred_element_type=F32
        )
        * scale
        for c in every
    ]
    masked = [jnp.where(valid[c], scores[c], -1e30) for c in every]
    peak = [jnp.maximum(jnp.max(masked[c], axis=1, keepdims=True), fresh[c]) for c in every]
    weights = [
        jnp.where(valid[c], jnp.exp(masked[c] - peak[c]), 0.0).astype(BF16) for c in every
    ]
    fresh_weight = [jnp.where(owner, jnp.exp(fresh[c] - peak[c]), 0.0) for c in every]
    total = [
        jnp.sum(weights[c].astype(F32), axis=1, keepdims=True) + fresh_weight[c] for c in every
    ]
    loads["values"].wait()
    load("hid", hid_hbm, hid)
    load("g1", g1_hbm, g1)
    load("rt1", rt1_hbm, rt1)
    load("id1", id1_hbm, id1)
    load("gu1", gu1_hbm.at[0], gu1)
    load("dn1", dn1_hbm.at[0], dn1)
    load("tp", tp_hbm, tp)
    load("g2", g2_hbm, g2)
    load("rt2", rt2_hbm, rt2)
    load("id2", id2_hbm, id2)
    load("gu2", gu2_hbm.at[0], gu2)
    load("dn2", dn2_hbm.at[0], dn2)
    mixed = [jnp.dot(weights[c], vbuf[c], preferred_element_type=F32) for c in every]
    for c in every:
        some = total[c] > 0.0
        safe = jnp.where(some, total[c], 1.0)
        lse = jnp.broadcast_to(jnp.where(some, peak[c] + jnp.log(safe), -1e30), (H, HD))
        whole = (mixed[c] + fresh_weight[c] * nkv[1, c : c + 1, :].astype(F32)) * (1.0 / safe)
        own = whole[:, 0:HD]
        for g in range(1, KVH):
            own = jnp.where(head_group == g, whole[:, g * HD : (g + 1) * HD], own)
        for t in range(nseq):
            o_stage[t, c * hp : (c + 1) * hp, :] = own[t * hp : (t + 1) * hp]
            l_stage[t, c * hp : (c + 1) * hp, :] = lse[t * hp : (t + 1) * hp]

    ar = count * hp
    diag = lax.broadcasted_iota(jnp.int32, (ar, HD), 0) == lax.broadcasted_iota(jnp.int32, (ar, HD), 1)
    part_row = lax.broadcasted_iota(jnp.int32, (RB, HD), 0)
    for t in range(nseq):
        att_send[t, 0:ar, :] = o_stage[t].astype(BF16)
        line = jnp.sum(jnp.where(diag, l_stage[t], 0.0), axis=0, keepdims=True)
        high = line.astype(BF16).astype(F32)
        mid = (line - high).astype(BF16).astype(F32)
        low = line - high - mid
        parts = jnp.where(part_row == 0, high, jnp.where(part_row == 1, mid, jnp.where(part_row == 2, low, 0.0)))
        att_send[t, ar : ar + RB, :] = parts.astype(BF16)
    pl.semaphore_wait(barrier, nseq + nexp - 2)
    scatter(att_send, att_recv, 0, s_me, along_seq, nseq, 0)
    lses = []
    for t in range(nseq):
        parts = att_recv[t, ar : ar + RB, :].astype(F32)
        line = parts[0:1] + parts[1:2] + parts[2:3]
        lses.append(jnp.sum(jnp.where(diag, line, 0.0), axis=1, keepdims=True))
    top = functools.reduce(jnp.maximum, lses)
    shares = [jnp.exp(x - top) for x in lses]
    norm = 1.0 / functools.reduce(jnp.add, shares)
    attn = functools.reduce(
        jnp.add, [att_recv[t, 0:ar, :].astype(F32) * (shares[t] * norm) for t in range(nseq)]
    )
    att_stage[...] = attn
    heads = jnp.concatenate(
        [att_stage[pl.ds(j, count, stride=hp), :] for j in range(hp)], axis=1
    ).astype(BF16)

    loads["wo"].wait()
    wide = 128 * stack
    half = d // wide // 2
    for i in range(d // wide):
        term = jnp.dot(heads, wo[:, i * wide : (i + 1) * wide], preferred_element_type=F32)
        terms[s_me, i] = pack(term)[0]
        if (i + 1) % half == 0:
            for k in range(1, nseq):
                own = terms.at[s_me, pl.ds(i + 1 - half, half)]
                remote(own, own, 1, along_seq(k)).start()
    await_bytes(terms.at[pl.ds(0, nseq - 1)], recv_sem.at[1])
    loads["hid"].wait()
    loads["g1"].wait()
    state = hid[...] + unpack(summed(terms, nseq))

    def experts(xn, router, ids, gu, dn, inner, rep, got, phase, width, hidden):
        gate = own_gate(xn, router, ids, me)
        step = 256 if hidden % 256 == 0 else 128
        for i in range(hidden // step):
            a = column_dot(xn, gu, i * step, step)
            b = column_dot(xn, gu, hidden + i * step, step)
            inner[:, i * step : (i + 1) * step] = (a * jax.nn.sigmoid(a) * b).astype(BF16)
        for i in range(width // wide):
            y = column_dot(inner, dn, i * wide, wide).astype(BF16).astype(F32)
            y = jnp.where(gate > 0.0, gate * y, 0.0)
            for e in range(nexp):
                rep[e, i] = pack(y[e * count : (e + 1) * count])[0]
            if (i + 1) % 2 == 0:
                for k in range(1, nexp):
                    dev = along_exp(k)
                    piece = pl.ds(i - 1, 2)
                    remote(rep.at[dev[1], piece], got.at[e_me, piece], phase, dev).start()
        got[e_me] = rep[e_me]
        await_bytes(got.at[pl.ds(0, nexp - 1)], recv_sem.at[phase])

    def layer(stream, gain, everyone, xn, router, ids, gu, dn, inner, rep, got, part, phase, names):
        for i, tile in enumerate(pack(normalise(stream, gain).astype(F32))):
            everyone[e_me, i] = tile
        gather(everyone, phase, e_me, along_exp, nexp)
        all_rows(everyone, xn)
        for name in names:
            loads[name].wait()
        experts(xn, router, ids, gu, dn, inner, rep, got, phase + 1, stream.shape[1], inner.shape[1])
        for i, tile in enumerate(summed(got, nexp)):
            part[s_me, i] = tile.astype(BF16)
        gather(part, phase + 2, s_me, along_seq, nseq)
        return stream + unpack(summed(part, nseq))

    thinker = layer(
        state, g1[...], state_all, xn1, rt1, id1, gu1, dn1, inner1, rep1, got1, part1, 2,
        ("rt1", "id1", "gu1", "dn1"),
    )
    out1_ref[...] = thinker
    loads["tp"].wait()
    loads["g2"].wait()
    thinker_bf = thinker.astype(BF16)
    talk_in = jnp.concatenate(
        [
            jnp.dot(thinker_bf, tp[:, i * wide : (i + 1) * wide], preferred_element_type=F32)
            for i in range(dt // wide)
        ],
        axis=1,
    )
    out2_ref[...] = layer(
        talk_in, g2[...], talk_all, xn2, rt2, id2, gu2, dn2, inner2, rep2, got2, part2, 5,
        ("rt2", "id2", "gu2", "dn2"),
    )

    for phase, buf, ways in (
        (0, att_send, nseq),
        (1, terms, nseq),
        (2, state_all, nexp),
        (3, rep1, nexp),
        (4, part1, nseq),
        (5, talk_all, nexp),
        (6, rep2, nexp),
        (7, part2, nseq),
    ):
        await_bytes(buf.at[pl.ds(0, ways - 1)], send_sem.at[phase])


def hand_over(from1, from2, to1, to2, sem):
    first = pltpu.make_async_copy(from1, to1, sem.at[0])
    second = pltpu.make_async_copy(from2, to2, sem.at[1])
    first.start()
    second.start()
    first.wait()
    second.wait()


def on_device(
    queries, new_kv, kv_cache, lengths, out_proj, hidden_in, norm_gain, router, expert_ids,
    w_gate_up, w_down, talk_proj, talk_gain, talk_router, talk_ids, talk_gate_up, talk_down,
):
    nseq, nexp = lax.axis_size("seq"), lax.axis_size("exp")
    count = queries.shape[0]
    span, kw = kv_cache.shape[2:]
    d, dt = talk_proj.shape
    ff, ft = w_down.shape[1], talk_down.shape[1]
    rows = nexp * count
    hp = H // nseq
    ar = count * hp
    wide = 128 * (RB // count)
    any_spec = pl.BlockSpec(memory_space=pl.ANY)
    vmem_spec = pl.BlockSpec(memory_space=pltpu.VMEM)
    args = (
        queries, new_kv, kv_cache, lengths, out_proj, hidden_in, norm_gain.reshape(1, d), router.T,
        expert_ids.T, w_gate_up, w_down, talk_proj, talk_gain.reshape(1, dt), talk_router.T,
        talk_ids.T, talk_gate_up, talk_down,
    )
    in_specs = [any_spec] * len(args)
    in_specs[3] = pl.BlockSpec(memory_space=pltpu.SMEM)
    own = lambda x, drop=0: pltpu.VMEM(x.shape[drop:], x.dtype)
    scratch = [
        own(args[0]), own(args[1]),
        pltpu.VMEM((count, span, kw), BF16), pltpu.VMEM((count, span, kw), BF16),
        own(args[4]), own(args[5]), own(args[6]), own(args[7]), own(args[8]),
        own(args[9], 1), own(args[10], 1), own(args[11]), own(args[12]), own(args[13]), own(args[14]),
        own(args[15], 1), own(args[16], 1),
        pltpu.VMEM((H * 8, HD), F32),
        pltpu.VMEM((nseq, ar, HD), F32), pltpu.VMEM((nseq, ar, HD), F32),
        pltpu.VMEM((nseq, ar + RB, HD), BF16), pltpu.VMEM((nseq, ar + RB, HD), BF16),
        pltpu.VMEM((ar, HD), F32),
        pltpu.VMEM((nseq, d // wide, RB, 128), BF16),
        pltpu.VMEM((nexp, d // wide, RB, 128), BF16),
        pltpu.VMEM((rows, d), BF16), pltpu.VMEM((rows, ff), BF16),
        pltpu.VMEM((nexp, d // wide, RB, 128), BF16), pltpu.VMEM((nexp, d // wide, RB, 128), BF16),
        pltpu.VMEM((nseq, d // wide, RB, 128), BF16),
        pltpu.VMEM((nexp, dt // wide, RB, 128), BF16),
        pltpu.VMEM((rows, dt), BF16), pltpu.VMEM((rows, ft), BF16),
        pltpu.VMEM((nexp, dt // wide, RB, 128), BF16), pltpu.VMEM((nexp, dt // wide, RB, 128), BF16),
        pltpu.VMEM((nseq, dt // wide, RB, 128), BF16),
        pltpu.SemaphoreType.DMA((17,)),
        pltpu.SemaphoreType.DMA((8,)),
        pltpu.SemaphoreType.DMA((8,)),
    ]
    outs = (
        jax.ShapeDtypeStruct((count, d), F32),
        jax.ShapeDtypeStruct((count, dt), F32),
    )
    both = pl.pallas_call(
        functools.partial(kernel, nseq, nexp),
        out_shape=outs,
        in_specs=in_specs,
        out_specs=(vmem_spec, vmem_spec),
        scratch_shapes=scratch,
        compiler_params=pltpu.CompilerParams(
            collective_id=0, has_side_effects=True, vmem_limit_bytes=56 * 1024 * 1024
        ),
    )(*args)
    return pl.pallas_call(
        hand_over,
        out_shape=outs,
        in_specs=[any_spec] * 2,
        out_specs=(any_spec, any_spec),
        scratch_shapes=[pltpu.SemaphoreType.DMA((2,))],
        compiler_params=pltpu.CompilerParams(vmem_limit_bytes=60 * 1024 * 1024),
    )(*both)


def solution(mesh):
    placed = (
        P("exp", None),
        P(None, "exp", None),
        P(None, "exp", "seq", None),
        P("exp"),
        P("seq", None),
        P("exp", None),
        P(),
        P(),
        P(),
        P(("seq", "exp"), None, None),
        P(("seq", "exp"), None, None),
        P(),
        P(),
        P(),
        P(),
        P(("seq", "exp"), None, None),
        P(("seq", "exp"), None, None),
    )
    return jax.shard_map(
        on_device,
        mesh=mesh,
        in_specs=placed,
        out_specs=(P("exp", None), P("exp", None)),
        check_vma=False,
    )
```
